256 devices in a mesh: dp: 16 (over x, z_hi), tensor: 16 (over y, z_lo, core).
Axes of the slice: x: 4, y: 4, z: 8 (z_hi: 4, z_lo: 2; z = z_hi * 2 + z_lo), core: 2. Of those that a mesh axis runs over, the one named last changes fastest.
Arguments:
- acts: bfloat16 [2048, 4096], P('dp', 'tensor'), may hold values from -6 to 6
- grads: bfloat16 [2048, 14336], P('dp', 'tensor'), may hold values from -6 to 6
- basis_in: bfloat16 [4096, 4096], P(None, 'tensor'), may hold values from -0.09375 to 0.09375
- basis_out: bfloat16 [14336, 14336], P('tensor', 'dp'), may hold values from -0.046875 to 0.046875
- scale_old: float32 [4096, 14336], P('tensor', 'dp'), may hold values from 0.25 to 4
Outputs:
- scale_new: float32 [4096, 14336], P('tensor', 'dp')
- step: bfloat16 [4096, 14336], P('dp', 'tensor')
The draws below stay inside these ranges and needn't reach their ends.
All inputs are finite; a program needn't handle non-finite values.
Results may differ from the reference program's by a relative error of at most 0.029.
Values may be sent and summed in bfloat16 or wider, within the bound.
No kernel may reach another device: no remote copies, remote signals or barrier semaphores. Data moves between devices by JAX's collectives and lax.ppermute only.
A program may use at most 64 MiB of HBM per device.

```python
import math
import jax
import jax.numpy as jnp
from jax import lax

D = 4096
FF = 14336
TOKENS = 2048
N_DP = 16
N_TENSOR = 16


def steps_of(key, shape, pieces, smallest, largest):
    def one(position, blocks):
        heights = jax.random.uniform(jax.random.fold_in(jax.random.fold_in(key, 6), position), (blocks,), jnp.float32, smallest / len(pieces), largest / len(pieces))
        return jnp.repeat(jnp.exp(heights), shape[position] // blocks).reshape((-1,) + (1,) * (len(shape) - position - 1))

    gain = one(*pieces[0])
    for cut in pieces[1:]:
        gain = gain * one(*cut)
    return gain


def noise(rng, dims, deviation, reach, split=(), dtype=jnp.bfloat16):
    factor_of = steps_of(rng, dims, split, -0.22, 0.18) if split else 1.0
    values = jax.random.normal(rng, dims, jnp.float32) * deviation * factor_of
    return jnp.minimum(jnp.maximum(values, -reach), reach).astype(dtype)


def setup_inputs(seed: int = 0) -> dict:
    arg_keys = jax.random.split(jax.random.key(seed), 6)
    acts = noise(arg_keys[0], (TOKENS, D), 1.0, 6.0, ((0, 16), (1, 16)))
    grads = noise(arg_keys[1], (TOKENS, FF), 1.0, 6.0, ((0, 16), (1, 16)))
    basis_in = noise(arg_keys[2], (D, D), D ** -0.5, 0.09375, ((1, 16),))
    basis_out = noise(arg_keys[3], (FF, FF), FF ** -0.5, 0.046875, ((0, 16), (1, 16)))
    scale_old = jnp.clip(jnp.exp(math.log(4.0) - 2.7725887 * jax.random.uniform(arg_keys[4], (D, FF), jnp.float32) ** steps_of(arg_keys[4], (D, FF), ((0, 16), (1, 16)), -0.2, 0.2)), 0.25, 4.0)
    return {"acts": acts, "grads": grads, "basis_in": basis_in, "basis_out": basis_out, "scale_old": scale_old}


decay_rate = 0.5
damping = 0.1

def reference(acts, grads, basis_in, basis_out, scale_old):
    act_proj = jnp.dot(acts, basis_in, preferred_element_type=jnp.float32).astype(jnp.bfloat16)
    width_out = FF // N_TENSOR
    grad_total = jnp.zeros((TOKENS, FF), jnp.float32)
    for member in range(N_TENSOR):
        lower = member * width_out
        partial_value = jnp.dot(grads[:, lower:lower + width_out], basis_out[lower:lower + width_out, :], preferred_element_type=jnp.float32)
        grad_total = grad_total + lax.optimization_barrier(partial_value.astype(jnp.bfloat16)).astype(jnp.float32)
    grad_proj = grad_total.astype(jnp.bfloat16)
    act_wide = act_proj.astype(jnp.float32)
    grad_wide = grad_proj.astype(jnp.float32)
    act_square = (act_wide * act_wide).astype(jnp.bfloat16)
    grad_square = (grad_wide * grad_wide).astype(jnp.bfloat16)
    contract = (((0,), (0,)), ((), ()))
    window = lax.dot_general(act_square, grad_square, contract, preferred_element_type=jnp.float32) / TOKENS
    mean_grad = lax.dot_general(act_proj, grad_proj, contract, preferred_element_type=jnp.float32) / TOKENS
    scale_new = decay_rate * scale_old + (1.0 - decay_rate) * window
    corrected = (mean_grad / (scale_new + damping)).astype(jnp.bfloat16)
    width_in = D // N_TENSOR
    left_total = jnp.zeros((D, FF), jnp.float32)
    for member in range(N_TENSOR):
        lower = member * width_in
        partial_value = jnp.dot(basis_in[:, lower:lower + width_in], corrected[lower:lower + width_in, :], preferred_element_type=jnp.float32)
        left_total = left_total + lax.optimization_barrier(partial_value.astype(jnp.bfloat16)).astype(jnp.float32)
    left = left_total.astype(jnp.bfloat16)
    width_col = FF // N_DP
    update_total = jnp.zeros((D, FF), jnp.float32)
    for member in range(N_DP):
        lower = member * width_col
        partial_value = lax.dot_general(left[:, lower:lower + width_col], basis_out[:, lower:lower + width_col], (((1,), (1,)), ((), ())), preferred_element_type=jnp.float32)
        update_total = update_total + lax.optimization_barrier(partial_value.astype(jnp.bfloat16)).astype(jnp.float32)
    step = (-math.sqrt(TOKENS) * update_total).astype(jnp.bfloat16)
    return (scale_new, step)
```

```python
import math

import jax
import jax.numpy as jnp
from jax import lax
from jax.sharding import Mesh, PartitionSpec as P

decay_rate = 0.5
damping = 0.1
CHUNKS = 2
SIZES = {"x": 4, "zh": 4, "y": 4, "zl": 2, "c": 2}


def send(value, axes, target):
    if isinstance(axes, str):
        n = SIZES[axes]
        return lax.ppermute(value, axes, [(i, target(i) % n) for i in range(n)])
    n, m = SIZES[axes[0]], SIZES[axes[1]]
    pairs = [(i * m + j, (target(i, j) % n) * m + j) for i in range(n) for j in range(m)]
    return lax.ppermute(value, axes, pairs)


def swap(value, axis):
    return send(value, axis, lambda i: i + 1)


def roll(value, shift, axis):
    return lax.dynamic_slice_in_dim(
        jnp.concatenate([value, value], axis), shift % value.shape[axis], value.shape[axis], axis
    )


def total(values):
    result = values[0].astype(jnp.float32)
    for value in values[1:]:
        result = result + value.astype(jnp.float32)
    return result


def dot(a, b, dims=((1,), (0,))):
    return lax.dot_general(a, b, (dims, ((), ())), preferred_element_type=jnp.float32)


ZH = [(b, s) for b in range(2) for s in range(2)]


def reduce_t(pieces):
    got = [pieces[0]] + [send(pieces[j], "y", lambda i, j=j: i + j) for j in (1, 2, 3)]
    mine = total(got).astype(jnp.bfloat16)
    half = mine.shape[0] // 2
    return total([mine[:half], swap(mine[half:], "zl")]).astype(jnp.bfloat16)


def gather_t(piece):
    both = jnp.concatenate([piece, swap(piece, "zl")], 0)
    return [both] + [send(both, "y", lambda i, k=k: i + k) for k in (1, 2, 3)]


def body(acts, grads, basis_in, basis_out, scale_old):
    x, zh, y, zl, c = (lax.axis_index(a) for a in ("x", "zh", "y", "zl", "c"))
    bf16 = jnp.bfloat16

    halves = roll(grads.reshape(2, 64, 896), c, 0)
    grads_chip = jnp.concatenate([halves[0], swap(halves[1], "c")], 1)
    out_chip = jnp.concatenate([basis_out, swap(basis_out, "c")], 0)

    acts_all = lax.all_gather(acts, ("y", "zl", "c"), axis=1, tiled=True)

    line = jnp.concatenate(
        [send(grads_chip, ("zh", "zl"), lambda i, j, b=b, s=s: i + 2 * ((j + b) % 2) + s) for b, s in ZH], 0
    )
    terms = [
        dot(send(line, ("x", "y"), lambda i, k, j=j: i + k + j), out_chip).astype(bf16) for j in range(4)
    ]
    grad_half = jnp.concatenate(gather_t(reduce_t(terms)), 0)
    grad_proj = jnp.concatenate([grad_half, swap(grad_half, "c")], 0)

    act_local = roll(dot(acts_all, basis_in).astype(bf16).reshape(2, 64, 256), c, 0)
    act_line = jnp.concatenate(
        [send(act_local, ("zh", "zl"), lambda i, j, b=b, s=s: i + 2 * ((j + b) % 2) + s) for b, s in ZH], 1
    )
    act_proj = jnp.concatenate(
        [send(act_line, ("x", "y"), lambda i, j, k=k: i + j - k) for k in range(4)], 1
    ).reshape(2048, 256)

    act_square = act_proj * act_proj
    grad_square = grad_proj * grad_proj
    window = dot(act_square, grad_square, ((0,), (0,))) / 2048
    mean_grad = dot(act_proj, grad_proj, ((0,), (0,))) / 2048
    scale_new = decay_rate * scale_old + (1.0 - decay_rate) * window
    corrected = (mean_grad / (scale_new + damping)).astype(bf16)
    corrected_chip = jnp.concatenate([corrected, swap(corrected, "c")], 0)

    by_core = roll(basis_in.reshape(16, 2, 128, 256), c, 1)
    in_chip = jnp.concatenate([by_core[:, 0], swap(by_core[:, 1], "c")], 2).reshape(4, 4, 128, 512)
    in_chip = roll(roll(in_chip, x + y, 0), zh + 2 * zl, 1)

    width = 128 // CHUNKS
    steps = []
    for chunk in range(CHUNKS):
        rows = in_chip[:, :, chunk * width : (chunk + 1) * width].reshape(4, 4 * width, 512)
        left = gather_t(reduce_t([dot(rows[j], corrected_chip).astype(bf16) for j in range(4)]))
        update = total(
            [
                send(
                    dot(left[k], out_chip, ((1,), (1,))).astype(bf16),
                    ("x", "y"),
                    lambda i, j, k=k: i + j - k,
                )
                for k in range(4)
            ]
        ).astype(bf16)
        update = update.reshape(4, width, 1792)
        steps.append(
            total(
                [
                    send(update[n], ("zh", "zl"), lambda i, j, b=b, s=s: i + 2 * ((j + b) % 2) + s)
                    for n, (b, s) in enumerate(ZH)
                ]
            )
        )
    step = (-math.sqrt(2048) * jnp.concatenate(steps, 0)).astype(bf16)
    both = jnp.stack([step[:, :896], swap(step[:, 896:], "c")])
    return (scale_new, roll(both, c, 0).reshape(256, 896))


def solution(mesh):
    inner = Mesh(mesh.devices.reshape(4, 4, 4, 2, 2), ("x", "zh", "y", "zl", "c"))
    dp, tensor = ("x", "zh"), ("y", "zl", "c")
    return jax.shard_map(
        body,
        mesh=inner,
        in_specs=(P(dp, tensor), P(dp, tensor), P(None, tensor), P(tensor, dp), P(tensor, dp)),
        out_specs=(P(tensor, dp), P(dp, tensor)),
        check_vma=False,
    )
```

```python
import math

import jax
import jax.numpy as jnp
from jax import lax
from jax.sharding import Mesh, PartitionSpec as P

decay_rate = 0.5
damping = 0.1
SIZES = {"x": 4, "zh": 4, "y": 4, "zl": 2, "c": 2}
TOKEN_CHUNKS = 2
ROW_CHUNKS = 4
GROUPS = ((0, 1), (2,), (3,))
bf16 = jnp.bfloat16


def send(value, axes, target):
    if isinstance(axes, str):
        n = SIZES[axes]
        return lax.ppermute(value, axes, [(i, target(i) % n) for i in range(n)])
    n, m = SIZES[axes[0]], SIZES[axes[1]]
    pairs = [(i * m + j, (target(i, j) % n) * m + j) for i in range(n) for j in range(m)]
    return lax.ppermute(value, axes, pairs)


def swap(value, axis):
    return send(value, axis, lambda i: i + 1)


def along(value, axis, step):
    return send(value, axis, lambda i: i + step)


def after(value, token):
    return lax.optimization_barrier((value, token))[0]


def roll(value, shift, axis):
    return lax.dynamic_slice_in_dim(
        jnp.concatenate([value, value], axis), shift % value.shape[axis], value.shape[axis], axis
    )


def total(values):
    result = values[0].astype(jnp.float32)
    for value in values[1:]:
        result = result + value.astype(jnp.float32)
    return result


def dot(a, b, dims=((1,), (0,))):
    return lax.dot_general(a, b, (dims, ((), ())), preferred_element_type=jnp.float32)


def sum_y(pieces):
    got = [pieces[0]] + [along(pieces[j], "y", j) for j in (1, 2, 3)]
    return total(got).astype(bf16)


def sum_zl(piece):
    return total([piece, swap(piece, "zl")]).astype(bf16)


def gather_y(piece):
    return [piece] + [along(piece, "y", k) for k in (1, 2, 3)]


def body(acts, grads, basis_in, basis_out, scale_old):
    x, zh, y, zl, c = (lax.axis_index(a) for a in ("x", "zh", "y", "zl", "c"))

    halves = roll(grads.reshape(2, 64, 896), c, 0)
    grads_chip = jnp.concatenate([halves[0], swap(halves[1], "c")], 1)
    out_chip = jnp.concatenate([basis_out, swap(basis_out, "c")], 0)

    features = roll(jnp.stack([acts, swap(acts, "c")]), c, 0)
    features = roll(jnp.stack([features, swap(features, "zl")]), zl, 0).reshape(4, 128, 256)
    in_blocks = basis_in.reshape(4, 4, 256, 256)
    act_local = sum(
        dot(
            features if k == 0 else along(features, "y", -k),
            lax.dynamic_index_in_dim(in_blocks, (y + k) % 4, 0, keepdims=False),
            ((0, 2), (0, 1)),
        )
        for k in range(4)
    ).astype(bf16)
    count = TOKEN_CHUNKS
    width = 64 // count
    act_local = roll(act_local.reshape(2, 64, 256), c, 0).reshape(2 * count, width, 256)
    act_line = jnp.concatenate([act_local] + [along(act_local, "zh", o) for o in (1, 2, 3)], 1)
    act_proj = jnp.concatenate(
        [send(act_line, ("x", "y"), lambda i, j, k=k: i + j - k) for k in range(4)], 1
    ).reshape(2048, 256)

    grad_halves = []
    sums = []
    for m in range(count):
        part = grads_chip[m * width : (m + 1) * width]
        line = jnp.concatenate([part] + [along(part, "zh", o) for o in (1, 2, 3)], 0)
        terms = [
            dot(send(line, ("x", "y"), lambda i, k, j=j: i + k + j), out_chip).astype(bf16) for j in range(4)
        ]
        if m:
            terms = after(terms, sums[m - 1])
        sums.append(sum_y(terms))
        grad_halves += gather_y(sum_zl(sums[m]))
    grad_half = jnp.concatenate(grad_halves, 0)
    grad_proj = jnp.concatenate([grad_half, swap(grad_half, "c")], 0)

    act_square = act_proj * act_proj
    grad_square = grad_proj * grad_proj
    window = dot(act_square, grad_square, ((0,), (0,))) / 2048
    mean_grad = dot(act_proj, grad_proj, ((0,), (0,))) / 2048
    scale_new = decay_rate * scale_old + (1.0 - decay_rate) * window
    corrected = (mean_grad / (scale_new + damping)).astype(bf16)
    corrected_chip = jnp.concatenate([corrected, swap(corrected, "c")], 0)

    by_core = roll(basis_in.reshape(16, 2, 128, 256), c, 1)
    in_chip = jnp.concatenate([by_core[:, 0], swap(by_core[:, 1], "c")], 2).reshape(4, 4, 128, 512)
    in_chip = roll(roll(in_chip, x + y, 0), zh, 1)

    width = 128 // ROW_CHUNKS
    sums = []
    lines = []
    for n in range(ROW_CHUNKS):
        rows = in_chip[:, :, n * width : (n + 1) * width].reshape(4, 4 * width, 512)
        pieces = [dot(rows[j], corrected_chip).astype(bf16) for j in range(4)]
        if n:
            pieces = after(pieces, sums[n - 1])
        sums.append(sum_y(pieces))
        left = gather_y(sum_zl(sums[n]))
        update = total(
            [
                send(
                    dot(left[k], out_chip, ((1,), (1,))).astype(bf16),
                    ("x", "y"),
                    lambda i, j, k=k: i + j - k,
                )
                for k in range(4)
            ]
        ).astype(bf16)
        lines.append(update.reshape(4, width, 1792))
    steps = []
    for group in GROUPS:
        line = jnp.concatenate([lines[n] for n in group], 1)
        steps.append(total([line[0]] + [along(line[o], "zh", o) for o in (1, 2, 3)]))
    step = (-math.sqrt(2048) * jnp.concatenate(steps, 0)).astype(bf16)
    both = jnp.stack([step[:, :896], swap(step[:, 896:], "c")])
    return (scale_new, roll(both, c, 0).reshape(256, 896))


def solution(mesh):
    inner = Mesh(mesh.devices.reshape(4, 4, 4, 2, 2), ("x", "zh", "y", "zl", "c"))
    dp, tensor = ("x", "zh"), ("y", "zl", "c")
    return jax.shard_map(
        body,
        mesh=inner,
        in_specs=(P(dp, tensor), P(dp, tensor), P(None, tensor), P(tensor, dp), P(tensor, dp)),
        out_specs=(P(tensor, dp), P(dp, tensor)),
        check_vma=False,
    )
```

```python
import math

import jax
import jax.numpy as jnp
from jax import lax
from jax.sharding import Mesh, PartitionSpec as P

decay_rate = 0.5
damping = 0.1
SIZES = {"x": 4, "zh": 4, "y": 4, "zl": 2, "c": 2}
ROW_CHUNKS = 4
GROUPS = ((0, 1), (2,), (3,))
bf16 = jnp.bfloat16


def send(value, axes, target):
    if isinstance(axes, str):
        n = SIZES[axes]
        return lax.ppermute(value, axes, [(i, target(i) % n) for i in range(n)])
    n, m = SIZES[axes[0]], SIZES[axes[1]]
    pairs = [(i * m + j, (target(i, j) % n) * m + j) for i in range(n) for j in range(m)]
    return lax.ppermute(value, axes, pairs)


def swap(value, axis):
    return send(value, axis, lambda i: i + 1)


def along(value, axis, step):
    return send(value, axis, lambda i: i + step)


def after(value, token):
    return lax.optimization_barrier((value, token))[0]


def roll(value, shift, axis):
    return lax.dynamic_slice_in_dim(
        jnp.concatenate([value, value], axis), shift % value.shape[axis], value.shape[axis], axis
    )


def total(values):
    result = values[0].astype(jnp.float32)
    for value in values[1:]:
        result = result + value.astype(jnp.float32)
    return result


def dot(a, b, dims=((1,), (0,))):
    return lax.dot_general(a, b, (dims, ((), ())), preferred_element_type=jnp.float32)


def sum_y(pieces):
    got = [pieces[0]] + [along(pieces[j], "y", j) for j in (1, 2, 3)]
    return total(got).astype(bf16)


def sum_zl(piece):
    return total([piece, swap(piece, "zl")]).astype(bf16)


def gather_y(piece):
    return [piece] + [along(piece, "y", -k) for k in (1, 2, 3)]


def place(pieces, y):
    result = jnp.zeros((4,) + pieces[0].shape, pieces[0].dtype)
    for k, piece in enumerate(pieces):
        result = lax.dynamic_update_index_in_dim(result, piece, (y + k) % 4, 0)
    return result


def body(acts, grads, basis_in, basis_out, scale_old):
    x, zh, y, zl, c = (lax.axis_index(a) for a in ("x", "zh", "y", "zl", "c"))

    halves = roll(grads.reshape(2, 64, 896), c, 0)
    grads_chip = jnp.concatenate([halves[0], swap(halves[1], "c")], 1)
    out_chip = jnp.concatenate([basis_out, swap(basis_out, "c")], 0)

    features = roll(jnp.stack([acts, swap(acts, "c")]), c, 0)
    features = roll(jnp.stack([features, swap(features, "zl")]), zl, 0).reshape(4, 128, 256)
    in_blocks = basis_in.reshape(4, 4, 256, 256)
    act_local = sum(
        dot(
            features if k == 0 else along(features, "y", -k),
            lax.dynamic_index_in_dim(in_blocks, (y + k) % 4, 0, keepdims=False),
            ((0, 2), (0, 1)),
        )
        for k in range(4)
    ).astype(bf16)
    act_local = roll(act_local.reshape(2, 64, 256), c, 0)
    act_local = jnp.concatenate([act_local[0], act_local[1]], 1)

    line = jnp.concatenate([grads_chip] + [along(grads_chip, "zh", o) for o in (1, 2, 3)], 0)
    act_line = jnp.concatenate([act_local] + [along(act_local, "zh", o) for o in (1, 2, 3)], 0)
    tokens = lax.all_gather(jnp.concatenate([line, act_line], 1), "x", axis=0)
    terms = [
        dot(lax.dynamic_index_in_dim(tokens, (y + j) % 4, 0, keepdims=False)[:, :1792], out_chip).astype(bf16)
        for j in range(4)
    ]
    grad_half = place(gather_y(sum_zl(sum_y(terms))), y).reshape(1024, 896)
    grad_parts = (grad_half, swap(grad_half, "c"))
    act_parts = [tokens[:, :, n : n + 256].reshape(1024, 256) for n in (1792, 2048)]

    def contract(left, right):
        return sum(dot(a, b, ((0,), (0,))) for a, b in zip(left, right)) / 2048

    window = contract([a * a for a in act_parts], [g * g for g in grad_parts])
    mean_grad = contract(act_parts, grad_parts)
    scale_new = decay_rate * scale_old + (1.0 - decay_rate) * window
    corrected = (mean_grad / (scale_new + damping)).astype(bf16)
    corrected_chip = jnp.concatenate([corrected, swap(corrected, "c")], 0)

    by_core = roll(basis_in.reshape(16, 2, 128, 256), c, 1)
    in_chip = jnp.concatenate([by_core[:, 0], swap(by_core[:, 1], "c")], 2).reshape(4, 4, 128, 512)
    in_chip = roll(roll(in_chip, y, 0), zh, 1)

    width = 128 // ROW_CHUNKS
    sums = []
    lines = []
    for n in range(ROW_CHUNKS):
        rows = in_chip[:, :, n * width : (n + 1) * width].reshape(4, 4 * width, 512)
        pieces = [dot(rows[j], corrected_chip).astype(bf16) for j in range(4)]
        if n:
            pieces = after(pieces, sums[n - 1])
        sums.append(sum_y(pieces))
        left = place(gather_y(sum_zl(sums[n])), y).reshape(16 * width, 896)
        update = dot(left, out_chip, ((1,), (1,))).astype(bf16)
        update = lax.psum_scatter(update, "x", scatter_dimension=0, tiled=True)
        lines.append(update.reshape(4, width, 1792))
    steps = []
    for group in GROUPS:
        line = jnp.concatenate([lines[n] for n in group], 1)
        steps.append(total([line[0]] + [along(line[o], "zh", o) for o in (1, 2, 3)]))
    step = (-math.sqrt(2048) * jnp.concatenate(steps, 0)).astype(bf16)
    both = jnp.stack([step[:, :896], swap(step[:, 896:], "c")])
    return (scale_new, roll(both, c, 0).reshape(256, 896))


def solution(mesh):
    inner = Mesh(mesh.devices.reshape(4, 4, 4, 2, 2), ("x", "zh", "y", "zl", "c"))
    dp, tensor = ("x", "zh"), ("y", "zl", "c")
    return jax.shard_map(
        body,
        mesh=inner,
        in_specs=(P(dp, tensor), P(dp, tensor), P(None, tensor), P(tensor, dp), P(tensor, dp)),
        out_specs=(P(tensor, dp), P(dp, tensor)),
        check_vma=False,
    )
```

```python
import math

import jax
import jax.numpy as jnp
from jax import lax
from jax.sharding import Mesh, PartitionSpec as P

decay_rate = 0.5
damping = 0.1
SIZES = {"x": 4, "zh": 4, "y": 4, "zl": 2, "c": 2}
WIDTHS = (32, 48, 48)
bf16 = jnp.bfloat16


def send(value, axes, target):
    if isinstance(axes, str):
        n = SIZES[axes]
        return lax.ppermute(value, axes, [(i, target(i) % n) for i in range(n)])
    n, m = SIZES[axes[0]], SIZES[axes[1]]
    pairs = [(i * m + j, (target(i, j) % n) * m + j) for i in range(n) for j in range(m)]
    return lax.ppermute(value, axes, pairs)


def swap(value, axis):
    return send(value, axis, lambda i: i + 1)


def along(value, axis, step):
    return send(value, axis, lambda i: i + step)


def after(value, token):
    return lax.optimization_barrier((value, token))[0]


def roll(value, shift, axis):
    return lax.dynamic_slice_in_dim(
        jnp.concatenate([value, value], axis), shift % value.shape[axis], value.shape[axis], axis
    )


def total(values):
    result = values[0].astype(jnp.float32)
    for value in values[1:]:
        result = result + value.astype(jnp.float32)
    return result


def dot(a, b, dims=((1,), (0,))):
    return lax.dot_general(a, b, (dims, ((), ())), preferred_element_type=jnp.float32)


def sum_y(pieces):
    got = [pieces[0]] + [along(pieces[j], "y", j) for j in (1, 2, 3)]
    return total(got).astype(bf16)


def sum_zl(piece):
    return total([piece, swap(piece, "zl")]).astype(bf16)


def gather_y(piece):
    return [piece] + [along(piece, "y", k) for k in (1, 2, 3)]


def reduce_x(terms):
    return total([send(term, ("x", "y"), lambda i, j, k=k: i + j - k) for k, term in enumerate(terms)]).astype(bf16)


def body(acts, grads, basis_in, basis_out, scale_old):
    x, zh, y, zl, c = (lax.axis_index(a) for a in ("x", "zh", "y", "zl", "c"))

    halves = roll(grads.reshape(2, 64, 896), c, 0)
    grads_chip = jnp.concatenate([halves[0], swap(halves[1], "c")], 1)
    out_chip = jnp.concatenate([basis_out, swap(basis_out, "c")], 0)

    line = jnp.concatenate([grads_chip] + [along(grads_chip, "zh", o) for o in (1, 2, 3)], 0)

    acts = after(acts, line)
    features = roll(jnp.stack([acts, swap(acts, "c")]), c, 0)
    features = roll(jnp.stack([features, swap(features, "zl")]), zl, 0).reshape(4, 128, 256)
    in_blocks = basis_in.reshape(4, 4, 256, 256)
    act_local = sum(
        dot(
            features if k == 0 else along(features, "y", -k),
            lax.dynamic_index_in_dim(in_blocks, (y + k) % 4, 0, keepdims=False),
            ((0, 2), (0, 1)),
        )
        for k in range(4)
    ).astype(bf16)
    act_local = roll(act_local.reshape(2, 64, 256), c, 0)
    act_line = jnp.concatenate([act_local] + [along(act_local, "zh", o) for o in (1, 2, 3)], 1)

    terms = [
        dot(send(line, ("x", "y"), lambda i, k, j=j: i + k + j), out_chip).astype(bf16) for j in range(4)
    ]
    act_line = after(act_line, terms)
    act_proj = jnp.concatenate(
        [send(act_line, ("x", "y"), lambda i, j, k=k: i + j - k) for k in range(4)], 1
    ).reshape(2048, 256)
    grad_half = jnp.concatenate(gather_y(sum_zl(sum_y(terms))), 0)
    grad_proj = jnp.concatenate([grad_half, swap(grad_half, "c")], 0)

    act_square = act_proj * act_proj
    grad_square = grad_proj * grad_proj
    window = dot(act_square, grad_square, ((0,), (0,))) / 2048
    mean_grad = dot(act_proj, grad_proj, ((0,), (0,))) / 2048
    scale_new = decay_rate * scale_old + (1.0 - decay_rate) * window
    corrected = (mean_grad / (scale_new + damping)).astype(bf16)
    corrected_chip = jnp.concatenate([corrected, swap(corrected, "c")], 0)

    by_core = roll(basis_in.reshape(16, 2, 128, 256), c, 1)
    in_chip = jnp.concatenate([by_core[:, 0], swap(by_core[:, 1], "c")], 2).reshape(4, 4, 128, 512)
    in_chip = roll(roll(in_chip, x + y, 0), zh, 1)

    chunks = range(len(WIDTHS))
    pieces = []
    begin = 0
    for width in WIDTHS:
        rows = in_chip[:, :, begin : begin + width].reshape(4, 4 * width, 512)
        pieces.append([dot(rows[j], corrected_chip).astype(bf16) for j in range(4)])
        begin += width

    summed = [sum_y(pieces[0])]
    updates = []
    steps = []
    for n in chunks:
        if n == 0:
            pieces[1] = after(pieces[1], summed[0])
            summed.append(sum_y(pieces[1]))
        piece = sum_zl(summed[n])
        if n:
            piece, updates[n - 1] = lax.optimization_barrier((piece, updates[n - 1]))
            updates[n - 1] = reduce_x(updates[n - 1])
        left = gather_y(piece)
        updates.append([dot(left[k], out_chip, ((1,), (1,))).astype(bf16) for k in range(4)])
        if n + 2 in chunks:
            pieces[n + 2], updates[n] = lax.optimization_barrier((pieces[n + 2], updates[n]))
            summed.append(sum_y(pieces[n + 2]))
    updates[-1] = reduce_x(updates[-1])
    for n in chunks:
        line = updates[n].reshape(4, WIDTHS[n], 1792)
        steps.append(total([line[0]] + [along(line[o], "zh", o) for o in (1, 2, 3)]))
    step = (-math.sqrt(2048) * jnp.concatenate(steps, 0)).astype(bf16)
    both = jnp.stack([step[:, :896], swap(step[:, 896:], "c")])
    return (scale_new, roll(both, c, 0).reshape(256, 896))


def solution(mesh):
    inner = Mesh(mesh.devices.reshape(4, 4, 4, 2, 2), ("x", "zh", "y", "zl", "c"))
    dp, tensor = ("x", "zh"), ("y", "zl", "c")
    return jax.shard_map(
        body,
        mesh=inner,
        in_specs=(P(dp, tensor), P(dp, tensor), P(None, tensor), P(tensor, dp), P(tensor, dp)),
        out_specs=(P(tensor, dp), P(dp, tensor)),
        check_vma=False,
    )
```

```python
import math

import jax
import jax.numpy as jnp
from jax import lax
from jax.sharding import Mesh, PartitionSpec as P

decay_rate = 0.5
damping = 0.1
SIZES = {"x": 4, "zh": 4, "y": 4, "zl": 2, "c": 2}
TOKEN_CHUNKS = 2
WIDTHS = (64, 64)
bf16 = jnp.bfloat16


def swap(value):
    return lax.ppermute(value, "c", [(0, 1), (1, 0)])


def after(value, token):
    return lax.optimization_barrier((value, token))[0]


def roll(value, shift, axis):
    return lax.dynamic_slice_in_dim(
        jnp.concatenate([value, value], axis), shift % value.shape[axis], value.shape[axis], axis
    )


def dot(a, b, dims=((1,), (0,))):
    return lax.dot_general(a, b, (dims, ((), ())), preferred_element_type=jnp.float32)


def count(axes):
    return math.prod(SIZES[axis] for axis in axes)


def gather(value, axes):
    copies = jnp.broadcast_to(value[None], (count(axes),) + value.shape)
    return lax.all_to_all(copies, axes, 0, 0, tiled=True)


def reduce(value, axes):
    got = lax.all_to_all(value, axes, 0, 0, tiled=True)
    got = got.reshape((count(axes), -1) + value.shape[1:])
    return jnp.sum(got.astype(jnp.float32), 0).astype(bf16)


def body(acts, grads, basis_in, basis_out, scale_old):
    c = lax.axis_index("c")
    around = ("y", "zl")

    halves = roll(grads.reshape(2, 64, 896), c, 0)
    grads_chip = jnp.concatenate([halves[0], swap(halves[1])], 1)
    out_chip = jnp.concatenate([basis_out, swap(basis_out)], 0)

    width = 64 // TOKEN_CHUNKS
    lines = [
        lax.all_gather(grads_chip[m * width : (m + 1) * width], ("x", "zh"), axis=0, tiled=True)
        for m in range(TOKEN_CHUNKS)
    ]

    features = gather(acts, ("y", "zl", "c"))
    act_local = dot(features, basis_in.reshape(16, 256, 256), ((0, 2), (0, 1))).astype(bf16)
    act_local = roll(act_local.reshape(2, 64, 256), c, 0).reshape(2, TOKEN_CHUNKS, width, 256)
    act_proj = gather(gather(act_local, ("zh",)), ("x",))
    act_proj = jnp.transpose(act_proj, (2, 3, 0, 1, 4, 5)).reshape(2048, 256)
    out_chip = after(out_chip, act_proj)

    own, other = [], []
    for line in lines:
        term = dot(line, out_chip).astype(bf16)
        own.append(gather(reduce(term, around), around).reshape(-1, 896))
        other.append(swap(own[-1]))
    grad_proj = jnp.concatenate(own + other, 0)

    act_square = act_proj * act_proj
    grad_square = grad_proj * grad_proj
    window = dot(act_square, grad_square, ((0,), (0,))) / 2048
    mean_grad = dot(act_proj, grad_proj, ((0,), (0,))) / 2048
    scale_new = decay_rate * scale_old + (1.0 - decay_rate) * window
    corrected = (mean_grad / (scale_new + damping)).astype(bf16)
    corrected_chip = jnp.concatenate([corrected, swap(corrected)], 0)

    by_core = roll(basis_in.reshape(16, 2, 128, 256), c, 1)
    in_chip = jnp.concatenate([by_core[:, 0], swap(by_core[:, 1])], 2)

    steps = []
    begin = 0
    for width in WIDTHS:
        rows = in_chip[:, begin : begin + width].reshape(16 * width, 512)
        begin += width
        piece = reduce(dot(rows, corrected_chip).astype(bf16), around)
        left = gather(piece, around).reshape(16 * width, 896)
        update = dot(left, out_chip, ((1,), (1,))).astype(bf16)
        steps.append(lax.psum_scatter(update, ("x", "zh"), scatter_dimension=0, tiled=True))
    step = (-math.sqrt(2048) * jnp.concatenate(steps, 0).astype(jnp.float32)).astype(bf16)
    both = jnp.stack([step[:, :896], swap(step[:, 896:])])
    return (scale_new, roll(both, c, 0).reshape(256, 896))


def solution(mesh):
    inner = Mesh(mesh.devices.reshape(4, 4, 4, 2, 2), ("x", "zh", "y", "zl", "c"))
    dp, tensor = ("x", "zh"), ("y", "zl", "c")
    return jax.shard_map(
        body,
        mesh=inner,
        in_specs=(P(dp, tensor), P(dp, tensor), P(None, tensor), P(tensor, dp), P(tensor, dp)),
        out_specs=(P(tensor, dp), P(dp, tensor)),
        check_vma=False,
    )
```

```python
import math

import jax
import jax.numpy as jnp
from jax import lax
from jax.sharding import Mesh, PartitionSpec as P

decay_rate = 0.5
damping = 0.1
SIZES = {"x": 4, "zh": 4, "y": 4, "zl": 2, "c": 2}
TOKEN_CHUNKS = 2
WIDTHS = (56, 40, 32)
bf16 = jnp.bfloat16


def swap(value):
    return lax.ppermute(value, "c", [(0, 1), (1, 0)])


def after(value, token):
    return lax.optimization_barrier((value, token))[0]


def roll(value, shift, axis):
    return lax.dynamic_slice_in_dim(
        jnp.concatenate([value, value], axis), shift % value.shape[axis], value.shape[axis], axis
    )


def dot(a, b, dims=((1,), (0,))):
    return lax.dot_general(a, b, (dims, ((), ())), preferred_element_type=jnp.float32)


def count(axes):
    return math.prod(SIZES[axis] for axis in axes)


def gather(value, axes):
    copies = jnp.broadcast_to(value[None], (count(axes),) + value.shape)
    return lax.all_to_all(copies, axes, 0, 0, tiled=True)


def reduce(value, axes, dtype=bf16):
    got = lax.all_to_all(value, axes, 0, 0, tiled=True)
    got = got.reshape((count(axes), -1) + value.shape[1:])
    return jnp.sum(got.astype(jnp.float32), 0).astype(dtype)


def body(acts, grads, basis_in, basis_out, scale_old):
    c = lax.axis_index("c")
    around = ("y", "zl")

    halves = roll(grads.reshape(2, 64, 896), c, 0)
    grads_chip = jnp.concatenate([halves[0], swap(halves[1])], 1)
    out_chip = jnp.concatenate([basis_out, swap(basis_out)], 0)

    width = 64 // TOKEN_CHUNKS
    line = gather(grads_chip, ("zh",))
    lines = [
        lax.all_gather(line[:, m * width : (m + 1) * width].reshape(4 * width, 1792), "x", axis=0, tiled=True)
        for m in range(TOKEN_CHUNKS)
    ]

    features = gather(after(acts, line), ("y", "zl", "c"))
    act_local = dot(features, basis_in.reshape(16, 256, 256), ((0, 2), (0, 1))).astype(bf16)
    act_local = roll(act_local.reshape(2, 64, 256), c, 0).reshape(2, TOKEN_CHUNKS, width, 256)
    act_line = gather(act_local, ("zh",))
    out_chip = after(out_chip, act_line)
    act_proj = lax.all_gather(act_line.reshape(512, 256), "x", axis=0)
    act_proj = act_proj.reshape(4, 4, 2, TOKEN_CHUNKS, width, 256)
    act_proj = jnp.transpose(act_proj, (2, 3, 0, 1, 4, 5)).reshape(2048, 256)

    own, other = [], []
    for line in lines:
        term = dot(line, out_chip).astype(bf16)
        own.append(gather(reduce(term, around), around).reshape(-1, 896))
        other.append(swap(own[-1]))
    grad_proj = jnp.concatenate(own + other, 0)

    act_square = act_proj * act_proj
    grad_square = grad_proj * grad_proj
    window = dot(act_square, grad_square, ((0,), (0,))) / 2048
    mean_grad = dot(act_proj, grad_proj, ((0,), (0,))) / 2048
    scale_new = decay_rate * scale_old + (1.0 - decay_rate) * window
    corrected = (mean_grad / (scale_new + damping)).astype(bf16)
    corrected_chip = jnp.concatenate([corrected, swap(corrected)], 0)

    by_core = roll(basis_in.reshape(16, 2, 128, 256), c, 1)
    in_chip = jnp.concatenate([by_core[:, 0], swap(by_core[:, 1])], 2)

    steps = []
    begin = 0
    for width in WIDTHS:
        rows = in_chip[:, begin : begin + width].reshape(16 * width, 512)
        begin += width
        piece = reduce(dot(rows, corrected_chip).astype(bf16), around)
        left = gather(piece, around).reshape(16 * width, 896)
        update = dot(left, out_chip, ((1,), (1,))).astype(bf16)
        update = lax.psum_scatter(update, "x", scatter_dimension=0, tiled=True)
        steps.append(reduce(update, ("zh",), jnp.float32))
    step = (-math.sqrt(2048) * jnp.concatenate(steps, 0)).astype(bf16)
    both = jnp.stack([step[:, :896], swap(step[:, 896:])])
    return (scale_new, roll(both, c, 0).reshape(256, 896))


def solution(mesh):
    inner = Mesh(mesh.devices.reshape(4, 4, 4, 2, 2), ("x", "zh", "y", "zl", "c"))
    dp, tensor = ("x", "zh"), ("y", "zl", "c")
    return jax.shard_map(
        body,
        mesh=inner,
        in_specs=(P(dp, tensor), P(dp, tensor), P(None, tensor), P(tensor, dp), P(tensor, dp)),
        out_specs=(P(tensor, dp), P(dp, tensor)),
        check_vma=False,
    )
```

```python
import math

import jax
import jax.numpy as jnp
from jax import lax
from jax.sharding import Mesh, PartitionSpec as P

decay_rate = 0.5
damping = 0.1
SIZES = {"x": 4, "zh": 4, "y": 4, "zl": 2, "c": 2}
WIDTHS = (80, 48)
bf16 = jnp.bfloat16


def swap(value):
    return lax.ppermute(value, "c", [(0, 1), (1, 0)])


def after(value, token):
    return lax.optimization_barrier((value, token))[0]


def roll(value, shift, axis):
    return lax.dynamic_slice_in_dim(
        jnp.concatenate([value, value], axis), shift % value.shape[axis], value.shape[axis], axis
    )


def dot(a, b, dims=((1,), (0,))):
    return lax.dot_general(a, b, (dims, ((), ())), preferred_element_type=jnp.float32)


def count(axes):
    return math.prod(SIZES[axis] for axis in axes)


def gather(value, axes):
    copies = jnp.broadcast_to(value[None], (count(axes),) + value.shape)
    return lax.all_to_all(copies, axes, 0, 0, tiled=True)


def reduce(value, axes, dtype=bf16):
    got = lax.all_to_all(value, axes, 0, 0, tiled=True)
    got = got.reshape((count(axes), -1) + value.shape[1:])
    return jnp.sum(got.astype(jnp.float32), 0).astype(dtype)


def body(acts, grads, basis_in, basis_out, scale_old):
    c = lax.axis_index("c")
    around = ("y", "zl")

    halves = roll(grads.reshape(2, 64, 896), c, 0)
    grads_chip = jnp.concatenate([halves[0], swap(halves[1])], 1)
    out_chip = jnp.concatenate([basis_out, swap(basis_out)], 0)

    features = lax.all_gather(acts, ("y", "zl", "c"), axis=1, tiled=True)
    act_local = roll(dot(features, basis_in).astype(bf16).reshape(2, 64, 256), c, 0)
    act_line = gather(act_local, ("zh",))

    line = after(gather(grads_chip, ("zh",)), act_local).reshape(256, 1792)
    line = lax.all_gather(line, "x", axis=0, tiled=True)
    act_proj = lax.all_gather(act_line.reshape(512, 256), "x", axis=0).reshape(4, 4, 2, 64, 256)
    act_proj = jnp.transpose(act_proj, (2, 0, 1, 3, 4)).reshape(2048, 256)

    piece = reduce(dot(line, after(out_chip, act_line)).astype(bf16), around)
    grad_half = gather(after(piece, act_proj), around).reshape(1024, 896)
    grad_proj = jnp.concatenate([grad_half, swap(grad_half)], 0)

    act_square = act_proj * act_proj
    grad_square = grad_proj * grad_proj
    window = dot(act_square, grad_square, ((0,), (0,))) / 2048
    mean_grad = dot(act_proj, grad_proj, ((0,), (0,))) / 2048
    scale_new = decay_rate * scale_old + (1.0 - decay_rate) * window
    corrected = (mean_grad / (scale_new + damping)).astype(bf16)
    corrected_chip = jnp.concatenate([corrected, swap(corrected)], 0)

    by_core = roll(basis_in.reshape(16, 2, 128, 256), c, 1)
    in_chip = jnp.concatenate([by_core[:, 0], swap(by_core[:, 1])], 2)

    steps = []
    begin = 0
    for width in WIDTHS:
        rows = in_chip[:, begin : begin + width].reshape(16 * width, 512)
        begin += width
        piece = reduce(dot(rows, corrected_chip).astype(bf16), around)
        left = gather(piece, around).reshape(16 * width, 896)
        update = dot(left, out_chip, ((1,), (1,))).astype(bf16)
        corrected_chip = after(corrected_chip, update)
        update = lax.psum_scatter(update, "x", scatter_dimension=0, tiled=True)
        steps.append(reduce(update, ("zh",), jnp.float32))
    step = (-math.sqrt(2048) * jnp.concatenate(steps, 0)).astype(bf16)
    both = jnp.stack([step[:, :896], swap(step[:, 896:])])
    return (scale_new, roll(both, c, 0).reshape(256, 896))


def solution(mesh):
    inner = Mesh(mesh.devices.reshape(4, 4, 4, 2, 2), ("x", "zh", "y", "zl", "c"))
    dp, tensor = ("x", "zh"), ("y", "zl", "c")
    return jax.shard_map(
        body,
        mesh=inner,
        in_specs=(P(dp, tensor), P(dp, tensor), P(None, tensor), P(tensor, dp), P(tensor, dp)),
        out_specs=(P(tensor, dp), P(dp, tensor)),
        check_vma=False,
    )
```

```python
import math

import jax
import jax.numpy as jnp
from jax import lax
from jax.sharding import Mesh, PartitionSpec as P

decay_rate = 0.5
damping = 0.1
SIZES = {"x": 4, "zh": 4, "y": 4, "zl": 2, "c": 2}
WIDTHS = (80, 48)
bf16 = jnp.bfloat16


def swap(value):
    return lax.ppermute(value, "c", [(0, 1), (1, 0)])


def after(value, token):
    return lax.optimization_barrier((value, token))[0]


def roll(value, shift, axis):
    return lax.dynamic_slice_in_dim(
        jnp.concatenate([value, value], axis), shift % value.shape[axis], value.shape[axis], axis
    )


def dot(a, b, dims=((1,), (0,))):
    return lax.dot_general(a, b, (dims, ((), ())), preferred_element_type=jnp.float32)


def count(axes):
    return math.prod(SIZES[axis] for axis in axes)


def gather(value, axes):
    copies = jnp.broadcast_to(value[None], (count(axes),) + value.shape)
    return lax.all_to_all(copies, axes, 0, 0, tiled=True)


def reduce(value, axes, dtype=bf16):
    got = lax.all_to_all(value, axes, 0, 0, tiled=True)
    got = got.reshape((count(axes), -1) + value.shape[1:])
    return jnp.sum(got.astype(jnp.float32), 0).astype(dtype)


def body(acts, grads, basis_in, basis_out, scale_old):
    c = lax.axis_index("c")
    around = ("y", "zl")

    halves = roll(grads.reshape(2, 64, 896), c, 0)
    grads_chip = jnp.concatenate([halves[0], swap(halves[1])], 1)
    out_chip = jnp.concatenate([basis_out, swap(basis_out)], 0)

    line = gather(grads_chip, ("zh",)).reshape(256, 1792)
    features = gather(after(acts, line), ("y", "zl", "c"))
    line = lax.all_gather(line, "x", axis=0, tiled=True)

    act_local = dot(features, basis_in.reshape(16, 256, 256), ((0, 2), (0, 1))).astype(bf16)
    act_line = gather(roll(act_local.reshape(2, 64, 256), c, 0), ("zh",))
    act_proj = lax.all_gather(act_line.reshape(512, 256), "x", axis=0).reshape(4, 4, 2, 64, 256)
    act_proj = jnp.transpose(act_proj, (2, 0, 1, 3, 4)).reshape(2048, 256)

    piece = reduce(dot(line, after(out_chip, act_line)).astype(bf16), around)
    grad_half = gather(after(piece, act_proj), around).reshape(1024, 896)
    grad_proj = jnp.concatenate([grad_half, swap(grad_half)], 0)

    act_square = act_proj * act_proj
    grad_square = grad_proj * grad_proj
    window = dot(act_square, grad_square, ((0,), (0,))) / 2048
    mean_grad = dot(act_proj, grad_proj, ((0,), (0,))) / 2048
    scale_new = decay_rate * scale_old + (1.0 - decay_rate) * window
    corrected = (mean_grad / (scale_new + damping)).astype(bf16)
    corrected_chip = jnp.concatenate([corrected, swap(corrected)], 0)

    by_core = roll(basis_in.reshape(16, 2, 128, 256), c, 1)
    in_chip = jnp.concatenate([by_core[:, 0], swap(by_core[:, 1])], 2)

    steps = []
    begin = 0
    for width in WIDTHS:
        rows = in_chip[:, begin : begin + width].reshape(16 * width, 512)
        begin += width
        piece = reduce(dot(rows, corrected_chip).astype(bf16), around)
        left = gather(piece, around).reshape(16 * width, 896)
        update = dot(left, out_chip, ((1,), (1,))).astype(bf16)
        corrected_chip = after(corrected_chip, update)
        update = lax.psum_scatter(update, "x", scatter_dimension=0, tiled=True)
        steps.append(reduce(update, ("zh",), jnp.float32))
    step = (-math.sqrt(2048) * jnp.concatenate(steps, 0)).astype(bf16)
    both = jnp.stack([step[:, :896], swap(step[:, 896:])])
    return (scale_new, roll(both, c, 0).reshape(256, 896))


def solution(mesh):
    inner = Mesh(mesh.devices.reshape(4, 4, 4, 2, 2), ("x", "zh", "y", "zl", "c"))
    dp, tensor = ("x", "zh"), ("y", "zl", "c")
    return jax.shard_map(
        body,
        mesh=inner,
        in_specs=(P(dp, tensor), P(dp, tensor), P(None, tensor), P(tensor, dp), P(tensor, dp)),
        out_specs=(P(tensor, dp), P(dp, tensor)),
        check_vma=False,
    )
```

```python
import math

import jax
import jax.numpy as jnp
from jax import lax
from jax.experimental import pallas as pl
from jax.experimental.pallas import tpu as pltpu
from jax.sharding import Mesh, PartitionSpec as P

decay_rate = 0.5
damping = 0.1
SIZES = {"x": 4, "zh": 4, "y": 4, "zl": 2, "c": 2}
WIDTHS = (80, 48)
bf16 = jnp.bfloat16


def swap(value):
    return lax.ppermute(value, "c", [(0, 1), (1, 0)])


def after(value, token):
    return lax.optimization_barrier((value, token))[0]


def roll(value, shift, axis):
    return lax.dynamic_slice_in_dim(
        jnp.concatenate([value, value], axis), shift % value.shape[axis], value.shape[axis], axis
    )


def dot(a, b, dims=((1,), (0,))):
    return lax.dot_general(a, b, (dims, ((), ())), preferred_element_type=jnp.float32)


def matmul(a, b, contract):
    rows, depth = a.shape
    columns = b.shape[1 - contract]
    tile = 256 if rows % 256 == 0 else 128

    def kernel(a_ref, b_ref, out_ref):
        out_ref[...] = dot(a_ref[...], b_ref[...], ((1,), (contract,))).astype(bf16)

    return pl.pallas_call(
        kernel,
        out_shape=jax.ShapeDtypeStruct((rows, columns), bf16),
        grid=(rows // tile,),
        in_specs=[pl.BlockSpec((tile, depth), lambda i: (i, 0)), pl.BlockSpec(b.shape, lambda i: (0, 0))],
        out_specs=pl.BlockSpec((tile, columns), lambda i: (i, 0)),
        compiler_params=pltpu.CompilerParams(vmem_limit_bytes=32 * 2**20),
        cost_estimate=pl.CostEstimate(
            flops=2 * rows * depth * columns,
            bytes_accessed=2 * (rows * depth + depth * columns + rows * columns),
            transcendentals=0,
        ),
    )(a, b)


def count(axes):
    return math.prod(SIZES[axis] for axis in axes)


def gather(value, axes):
    copies = jnp.broadcast_to(value[None], (count(axes),) + value.shape)
    return lax.all_to_all(copies, axes, 0, 0, tiled=True)


def reduce(value, axes, dtype=bf16):
    got = lax.all_to_all(value, axes, 0, 0, tiled=True)
    got = got.reshape((count(axes), -1) + value.shape[1:])
    return jnp.sum(got.astype(jnp.float32), 0).astype(dtype)


def body(acts, grads, basis_in, basis_out, scale_old):
    c = lax.axis_index("c")
    around = ("y", "zl")

    halves = roll(grads.reshape(2, 64, 896), c, 0)
    grads_chip = jnp.concatenate([halves[0], swap(halves[1])], 1)
    out_chip = jnp.concatenate([basis_out, swap(basis_out)], 0)

    line = gather(grads_chip, ("zh",)).reshape(256, 1792)
    features = gather(after(acts, line), ("y", "zl", "c"))
    line = lax.all_gather(line, "x", axis=0, tiled=True)

    act_local = dot(features, basis_in.reshape(16, 256, 256), ((0, 2), (0, 1))).astype(bf16)
    act_line = gather(roll(act_local.reshape(2, 64, 256), c, 0), ("zh",))
    act_proj = lax.all_gather(act_line.reshape(512, 256), "x", axis=0).reshape(4, 4, 2, 64, 256)
    act_proj = jnp.transpose(act_proj, (2, 0, 1, 3, 4)).reshape(2048, 256)

    piece = reduce(matmul(line, after(out_chip, act_line), 0), around)
    grad_half = after(gather(piece, around).reshape(1024, 896), act_proj)
    grad_proj = jnp.concatenate([grad_half, swap(grad_half)], 0)

    act_square = act_proj * act_proj
    grad_square = grad_proj * grad_proj
    window = dot(act_square, grad_square, ((0,), (0,))) / 2048
    mean_grad = dot(act_proj, grad_proj, ((0,), (0,))) / 2048
    scale_new = decay_rate * scale_old + (1.0 - decay_rate) * window
    corrected = (mean_grad / (scale_new + damping)).astype(bf16)
    corrected_chip = jnp.concatenate([corrected, swap(corrected)], 0)

    by_core = roll(basis_in.reshape(16, 2, 128, 256), c, 1)
    in_chip = jnp.concatenate([by_core[:, 0], swap(by_core[:, 1])], 2)

    steps = []
    begin = 0
    for width in WIDTHS:
        rows = in_chip[:, begin : begin + width].reshape(16 * width, 512)
        begin += width
        piece = reduce(dot(rows, corrected_chip).astype(bf16), around)
        left = gather(piece, around).reshape(16 * width, 896)
        update = matmul(left, out_chip, 1)
        corrected_chip = after(corrected_chip, update)
        update = lax.psum_scatter(update, "x", scatter_dimension=0, tiled=True)
        steps.append(reduce(update, ("zh",), jnp.float32))
    step = (-math.sqrt(2048) * jnp.concatenate(steps, 0)).astype(bf16)
    both = jnp.stack([step[:, :896], swap(step[:, 896:])])
    return (scale_new, roll(both, c, 0).reshape(256, 896))


def solution(mesh):
    inner = Mesh(mesh.devices.reshape(4, 4, 4, 2, 2), ("x", "zh", "y", "zl", "c"))
    dp, tensor = ("x", "zh"), ("y", "zl", "c")
    return jax.shard_map(
        body,
        mesh=inner,
        in_specs=(P(dp, tensor), P(dp, tensor), P(None, tensor), P(tensor, dp), P(tensor, dp)),
        out_specs=(P(tensor, dp), P(dp, tensor)),
        check_vma=False,
    )
```

```python
import math

import jax
import jax.numpy as jnp
from jax import lax
from jax.experimental import pallas as pl
from jax.experimental.pallas import tpu as pltpu
from jax.sharding import Mesh, PartitionSpec as P

decay_rate = 0.5
damping = 0.1
SIZES = {"x": 4, "zh": 4, "y": 4, "zl": 2, "c": 2}
WIDTHS = (80, 48)
bf16 = jnp.bfloat16


def swap(value):
    return lax.ppermute(value, "c", [(0, 1), (1, 0)])


def after(value, token):
    return lax.optimization_barrier((value, token))[0]


def roll(value, shift, axis):
    return lax.dynamic_slice_in_dim(
        jnp.concatenate([value, value], axis), shift % value.shape[axis], value.shape[axis], axis
    )


def dot(a, b, dims=((1,), (0,))):
    return lax.dot_general(a, b, (dims, ((), ())), preferred_element_type=jnp.float32)


def matmul(a, b, contract):
    rows, depth = a.shape
    columns = b.shape[1 - contract]
    tile = 256 if rows % 256 == 0 else 128

    def kernel(a_ref, b_ref, out_ref):
        out_ref[...] = dot(a_ref[...], b_ref[...], ((1,), (contract,))).astype(bf16)

    return pl.pallas_call(
        kernel,
        out_shape=jax.ShapeDtypeStruct((rows, columns), bf16),
        grid=(rows // tile,),
        in_specs=[pl.BlockSpec((tile, depth), lambda i: (i, 0)), pl.BlockSpec(b.shape, lambda i: (0, 0))],
        out_specs=pl.BlockSpec((tile, columns), lambda i: (i, 0)),
        compiler_params=pltpu.CompilerParams(vmem_limit_bytes=56 * 2**20),
        cost_estimate=pl.CostEstimate(
            flops=2 * rows * depth * columns,
            bytes_accessed=2 * (rows * depth + depth * columns + rows * columns),
            transcendentals=0,
        ),
    )(a, b)


def count(axes):
    return math.prod(SIZES[axis] for axis in axes)


def gather(value, axes):
    copies = jnp.broadcast_to(value[None], (count(axes),) + value.shape)
    return lax.all_to_all(copies, axes, 0, 0, tiled=True)


def reduce(value, axes, dtype=bf16):
    got = lax.all_to_all(value, axes, 0, 0, tiled=True)
    got = got.reshape((count(axes), -1) + value.shape[1:])
    return jnp.sum(got.astype(jnp.float32), 0).astype(dtype)


def body(acts, grads, basis_in, basis_out, scale_old):
    c = lax.axis_index("c")
    around = ("y", "zl")

    halves = roll(grads.reshape(2, 64, 896), c, 0)
    grads_chip = jnp.concatenate([halves[0], swap(halves[1])], 1)
    out_chip = jnp.concatenate([basis_out, swap(basis_out)], 0)

    line = gather(grads_chip, ("zh",)).reshape(256, 1792)
    features = gather(after(acts, line), ("y", "zl", "c"))
    line = lax.all_gather(line, "x", axis=0, tiled=True)

    act_local = dot(features, basis_in.reshape(16, 256, 256), ((0, 2), (0, 1))).astype(bf16)
    act_line = gather(roll(act_local.reshape(2, 64, 256), c, 0), ("x", "zh"))
    act_proj = jnp.transpose(act_line, (1, 0, 2, 3)).reshape(2048, 256)

    piece = reduce(matmul(line, after(out_chip, act_proj), 0), around)
    grad_half = gather(piece, around).reshape(1024, 896)
    grad_proj = jnp.concatenate([grad_half, swap(grad_half)], 0)

    act_square = act_proj * act_proj
    grad_square = grad_proj * grad_proj
    window = dot(act_square, grad_square, ((0,), (0,))) / 2048
    mean_grad = dot(act_proj, grad_proj, ((0,), (0,))) / 2048
    scale_new = decay_rate * scale_old + (1.0 - decay_rate) * window
    corrected = (mean_grad / (scale_new + damping)).astype(bf16)
    corrected_chip = jnp.concatenate([corrected, swap(corrected)], 0)

    by_core = roll(basis_in.reshape(16, 2, 128, 256), c, 1)
    in_chip = jnp.concatenate([by_core[:, 0], swap(by_core[:, 1])], 2)

    steps = []
    begin = 0
    for width in WIDTHS:
        rows = in_chip[:, begin : begin + width].reshape(16 * width, 512)
        begin += width
        piece = reduce(dot(rows, corrected_chip).astype(bf16), around)
        left = gather(piece, around).reshape(16 * width, 896)
        update = matmul(left, out_chip, 1)
        corrected_chip = after(corrected_chip, update)
        update = lax.psum_scatter(update, "x", scatter_dimension=0, tiled=True)
        steps.append(reduce(update, ("zh",), jnp.float32))
    step = (-math.sqrt(2048) * jnp.concatenate(steps, 0)).astype(bf16)
    both = jnp.stack([step[:, :896], swap(step[:, 896:])])
    return (scale_new, roll(both, c, 0).reshape(256, 896))


def solution(mesh):
    inner = Mesh(mesh.devices.reshape(4, 4, 4, 2, 2), ("x", "zh", "y", "zl", "c"))
    dp, tensor = ("x", "zh"), ("y", "zl", "c")
    return jax.shard_map(
        body,
        mesh=inner,
        in_specs=(P(dp, tensor), P(dp, tensor), P(None, tensor), P(tensor, dp), P(tensor, dp)),
        out_specs=(P(tensor, dp), P(dp, tensor)),
        check_vma=False,
    )
```

```python
import math

import jax
import jax.numpy as jnp
from jax import lax
from jax.experimental import pallas as pl
from jax.experimental.pallas import tpu as pltpu
from jax.sharding import Mesh, PartitionSpec as P

decay_rate = 0.5
damping = 0.1
SIZES = {"x": 4, "zh": 4, "y": 4, "zl": 2, "c": 2}
WIDTHS = (80, 48)
bf16 = jnp.bfloat16


def swap(value):
    return lax.ppermute(value, "c", [(0, 1), (1, 0)])


def after(value, token):
    return lax.optimization_barrier((value, token))[0]


def roll(value, shift, axis):
    return lax.dynamic_slice_in_dim(
        jnp.concatenate([value, value], axis), shift % value.shape[axis], value.shape[axis], axis
    )


def dot(a, b, dims=((1,), (0,))):
    return lax.dot_general(a, b, (dims, ((), ())), preferred_element_type=jnp.float32)


def matmul(a, b, contract):
    rows, depth = a.shape
    columns = b.shape[1 - contract]
    tile = 256 if rows % 256 == 0 else 128

    def kernel(a_ref, b_ref, out_ref):
        out_ref[...] = dot(a_ref[...], b_ref[...], ((1,), (contract,))).astype(bf16)

    return pl.pallas_call(
        kernel,
        out_shape=jax.ShapeDtypeStruct((rows, columns), bf16),
        grid=(rows // tile,),
        in_specs=[pl.BlockSpec((tile, depth), lambda i: (i, 0)), pl.BlockSpec(b.shape, lambda i: (0, 0))],
        out_specs=pl.BlockSpec((tile, columns), lambda i: (i, 0)),
        compiler_params=pltpu.CompilerParams(vmem_limit_bytes=32 * 2**20),
        cost_estimate=pl.CostEstimate(
            flops=2 * rows * depth * columns,
            bytes_accessed=2 * (rows * depth + depth * columns + rows * columns),
            transcendentals=0,
        ),
    )(a, b)


def count(axes):
    return math.prod(SIZES[axis] for axis in axes)


def gather(value, axes):
    copies = jnp.broadcast_to(value[None], (count(axes),) + value.shape)
    return lax.all_to_all(copies, axes, 0, 0, tiled=True)


def reduce(value, axes, dtype=bf16):
    got = lax.all_to_all(value, axes, 0, 0, tiled=True)
    got = got.reshape((count(axes), -1) + value.shape[1:])
    return jnp.sum(got.astype(jnp.float32), 0).astype(dtype)


def body(acts, grads, basis_in, basis_out, scale_old):
    c = lax.axis_index("c")
    around = ("y", "zl")

    halves = roll(grads.reshape(2, 64, 896), c, 0)
    grads_chip = jnp.concatenate([halves[0], swap(halves[1])], 1)
    out_chip = jnp.concatenate([basis_out, swap(basis_out)], 0)

    line = gather(grads_chip, ("zh",)).reshape(256, 1792)
    features = gather(after(acts, line), ("y", "zl", "c"))
    line = lax.all_gather(line, "x", axis=0, tiled=True)

    act_local = dot(features, basis_in.reshape(16, 256, 256), ((0, 2), (0, 1))).astype(bf16)
    act_line = gather(roll(act_local.reshape(2, 64, 256), c, 0), ("zh",))
    act_proj = lax.all_gather(act_line.reshape(512, 256), "x", axis=0).reshape(4, 4, 2, 64, 256)
    act_proj = jnp.transpose(act_proj, (2, 0, 1, 3, 4)).reshape(2048, 256)

    piece = reduce(matmul(line, after(out_chip, act_line), 0), around)
    grad_half = gather(after(piece, act_proj), around).reshape(1024, 896)
    grad_proj = jnp.concatenate([grad_half, swap(grad_half)], 0)

    act_square = act_proj * act_proj
    grad_square = grad_proj * grad_proj
    window = dot(act_square, grad_square, ((0,), (0,))) / 2048
    mean_grad = dot(act_proj, grad_proj, ((0,), (0,))) / 2048
    scale_new = decay_rate * scale_old + (1.0 - decay_rate) * window
    corrected = (mean_grad / (scale_new + damping)).astype(bf16)
    corrected_chip = jnp.concatenate([corrected, swap(corrected)], 0)

    by_core = roll(basis_in.reshape(16, 2, 128, 256), c, 1)
    in_chip = jnp.concatenate([by_core[:, 0], swap(by_core[:, 1])], 2)

    steps = []
    begin = 0
    for width in WIDTHS:
        rows = in_chip[:, begin : begin + width].reshape(16 * width, 512)
        begin += width
        piece = reduce(dot(rows, corrected_chip).astype(bf16), around)
        left = gather(piece, around).reshape(16 * width, 896)
        update = matmul(left, out_chip, 1)
        corrected_chip = after(corrected_chip, update)
        update = lax.psum_scatter(update, "x", scatter_dimension=0, tiled=True)
        steps.append(reduce(update, ("zh",), jnp.float32))
    step = (-math.sqrt(2048) * jnp.concatenate(steps, 0)).astype(bf16)
    both = jnp.stack([step[:, :896], swap(step[:, 896:])])
    return (scale_new, roll(both, c, 0).reshape(256, 896))


def solution(mesh):
    inner = Mesh(mesh.devices.reshape(4, 4, 4, 2, 2), ("x", "zh", "y", "zl", "c"))
    dp, tensor = ("x", "zh"), ("y", "zl", "c")
    return jax.shard_map(
        body,
        mesh=inner,
        in_specs=(P(dp, tensor), P(dp, tensor), P(None, tensor), P(tensor, dp), P(tensor, dp)),
        out_specs=(P(tensor, dp), P(dp, tensor)),
        check_vma=False,
    )
```
